512 devices in a mesh: row: 8 (over y), col: 16 (over z, core), rep: 4 (over x).
Axes of the slice: x: 4, y: 8, z: 8, core: 2. Of those that a mesh axis runs over, the one named last changes fastest.
Arguments:
- tokens: bfloat16 [2048, 6144], P(('rep', 'row'), 'col'), may hold values from -6 to 6
- up_weight: bfloat16 [6144, 12288], P('col', 'row'), may hold values from -0.078125 to 0.078125
- down_weight: bfloat16 [12288, 6144], P('row', 'col'), may hold values from -0.0546875 to 0.0546875
- out_grads: bfloat16 [2048, 6144], P(('rep', 'row'), 'col'), may hold values from -6 to 6
Outputs:
- block_out: bfloat16 [2048, 6144], P(('rep', 'row'), 'col')
- token_grads: bfloat16 [2048, 6144], P(('rep', 'row'), 'col')
- up_grads: bfloat16 [6144, 12288], P('col', 'row')
- down_grads: bfloat16 [12288, 6144], P('row', 'col')
The draws below stay inside these ranges and needn't reach their ends.
All inputs are finite; a program needn't handle non-finite values.
Results may differ from the reference program's by a relative error of at most 0.033.
Values may be sent and summed in bfloat16 or wider, within the bound.
No kernel may reach another device: no remote copies, remote signals or barrier semaphores. Data moves between devices by JAX's collectives and lax.ppermute only.
A program may use at most 64 MiB of HBM per device.

```python
import jax
import jax.numpy as jnp
from jax import lax

D = 6144
FF = 12288
TOKENS = 2048
N_ROW = 8
N_COL = 16
N_REP = 4


def levels(stream_key, shape, shards, smallest, high):
    level = 1.0
    for axis_at, blocks in shards:
        draws = jax.random.uniform(jax.random.fold_in(jax.random.fold_in(stream_key, 6), axis_at), (blocks,), jnp.float32, smallest / len(shards), high / len(shards))
        level = level * jnp.repeat(jnp.exp(draws), shape[axis_at] // blocks).reshape((-1,) + (1,) * (len(shape) - 1 - axis_at))
    return level


def scatter_about(stream_key, dims, spread, limit, shards=(), kind=jnp.bfloat16):
    level = levels(stream_key, dims, shards, -0.22, 0.18) if shards else 1.0
    array = jax.random.normal(stream_key, dims, jnp.float32) * spread * level
    return jnp.minimum(jnp.maximum(array, -limit), limit).astype(kind)


def setup_inputs(seed: int = 0) -> dict:
    streams_of = jax.random.split(jax.random.key(seed), 5)
    return {
        "tokens": scatter_about(streams_of[0], (TOKENS, D), 1.0, 6.0, ((0, 32), (1, 16))),
        "up_weight": scatter_about(streams_of[1], (D, FF), D ** -0.5, 0.078125, ((0, 16), (1, 8))),
        "down_weight": scatter_about(streams_of[2], (FF, D), FF ** -0.5, 0.0546875, ((0, 8), (1, 16))),
        "out_grads": scatter_about(streams_of[3], (TOKENS, D), 1.0, 6.0, ((0, 32), (1, 16))),
    }


def blocked_product(left, right, parts):
    width = left.shape[1] // parts

    def accumulate(total, index):
        start = (index * width).astype(jnp.int32)
        part_left = lax.dynamic_slice_in_dim(left, start, width, 1)
        part_right = lax.dynamic_slice_in_dim(right, start, width, 0)
        term = jnp.dot(part_left, part_right, preferred_element_type=jnp.float32).astype(jnp.bfloat16)
        term = lax.optimization_barrier(term)
        return (total + term.astype(jnp.float32), None)
    empty = jnp.zeros((left.shape[0], right.shape[1]), jnp.float32)
    total, _ = lax.scan(accumulate, empty, jnp.arange(parts, dtype=jnp.int32))
    return total

def reference(tokens, up_weight, down_weight, out_grads):
    hidden = blocked_product(tokens, up_weight, N_COL)
    activated = jax.nn.gelu(hidden).astype(jnp.bfloat16)
    block_out = blocked_product(activated, down_weight, N_ROW).astype(jnp.bfloat16)
    activated_grads = blocked_product(out_grads, down_weight.T, N_COL)
    _, pullback = jax.vjp(jax.nn.gelu, hidden)
    hidden_grads = pullback(activated_grads)[0].astype(jnp.bfloat16)
    token_grads = blocked_product(hidden_grads, up_weight.T, N_ROW).astype(jnp.bfloat16)
    up_grads = blocked_product(tokens.T, hidden_grads, N_REP).astype(jnp.bfloat16)
    down_grads = blocked_product(activated.T, out_grads, N_REP).astype(jnp.bfloat16)
    return (block_out, token_grads, up_grads, down_grads)
```

```python
import jax
import jax.numpy as jnp
from jax import lax
from jax.sharding import Mesh, PartitionSpec as P

bf16 = jnp.bfloat16
f32 = jnp.float32


def gelu_pullback(hidden, upstream):
    _, pullback = jax.vjp(jax.nn.gelu, hidden)
    return pullback(upstream)[0]


def dot(left, right, dims):
    return lax.dot_general(
        left, right, ((dims[:1], dims[1:]), ((), ())), preferred_element_type=f32
    ).astype(bf16)


def swap(x):
    return lax.ppermute(x, "core", [(0, 1), (1, 0)])


def exchange(x, axis):
    return lax.all_to_all(x, axis, 0, 0, tiled=False)


def gather(x, axis):
    n = lax.axis_size(axis)
    got = exchange(jnp.broadcast_to(x[None], (n,) + x.shape), axis)
    return got.reshape((n * x.shape[0],) + x.shape[1:])


def per_device(tokens, up_weight, down_weight, out_grads):
    core = lax.axis_index("core")
    rows, width = tokens.shape
    half = up_weight.shape[1] // 2
    n_row, n_z, n_rep = (lax.axis_size(a) for a in ("row", "z", "rep"))
    mine, theirs = core * half, (1 - core) * half

    up_own = lax.dynamic_slice_in_dim(up_weight, mine, half, 1)
    up_other = swap(lax.dynamic_slice_in_dim(up_weight, theirs, half, 1))
    down_own = lax.dynamic_slice_in_dim(down_weight, mine, half, 0)
    down_other = swap(lax.dynamic_slice_in_dim(down_weight, theirs, half, 0))
    up = jnp.concatenate([up_own, up_other], 0)
    down = jnp.concatenate([down_own, down_other], 1)

    gathered = gather(jnp.concatenate([tokens, out_grads], 1), "row")
    other = swap(gathered)
    tok = jnp.concatenate([gathered[:, :width], other[:, :width]], 1)
    og = jnp.concatenate([gathered[:, width:], other[:, width:]], 1)

    total = tok.shape[0]
    share = total // n_z
    partial = jnp.concatenate([dot(tok, up, (1, 0)), dot(og, down, (1, 1))], 1)
    terms = exchange(partial.reshape(n_z, share, 2 * half), "z")
    sums = jnp.sum(terms.astype(f32), 0)
    hidden, act_grads = sums[:, :half], sums[:, half:]
    act = jax.nn.gelu(hidden).astype(bf16)
    hid_grads = gelu_pullback(hidden, act_grads).astype(bf16)
    both = gather(jnp.concatenate([act, hid_grads], 1), "z")
    act, hid_grads = both[:, :half], both[:, half:]

    down_local = dot(act, og, (0, 0)).reshape(n_rep, half // n_rep, 2 * width)
    up_local = dot(tok, hid_grads, (0, 0)).reshape(2, n_rep, width // n_rep, half)
    up_local = jnp.swapaxes(up_local, 0, 1).reshape(n_rep, 2 * width // n_rep, half)
    local = jnp.concatenate([down_local, up_local], 1)
    grads = jnp.sum(exchange(local, "rep").astype(f32), 0).astype(bf16)
    part = half // n_rep
    piece = width // n_rep
    down_mine, down_send = grads[:part, :width], grads[:part, width:]
    up_mine, up_send = grads[part : part + piece], grads[part + piece :]
    down_got, up_got = swap(down_send), swap(up_send)
    first = core == 0
    down_pair = jnp.where(
        first, jnp.stack([down_mine, down_got]), jnp.stack([down_got, down_mine])
    )
    up_pair = jnp.where(
        first,
        jnp.concatenate([up_mine, up_got], 1),
        jnp.concatenate([up_got, up_mine], 1),
    )
    rep = lax.axis_index("rep")
    down_out = jnp.zeros((2, n_rep, part, width), bf16)
    up_out = jnp.zeros((n_rep, piece, 2 * half), bf16)
    for k in range(n_rep):
        if k:
            ring = [(i, (i + k) % n_rep) for i in range(n_rep)]
            down_k = lax.ppermute(down_pair, "rep", ring)
            up_k = lax.ppermute(up_pair, "rep", ring)
        else:
            down_k, up_k = down_pair, up_pair
        source = lax.rem(rep + n_rep - k, n_rep)
        down_out = lax.dynamic_update_slice_in_dim(down_out, down_k[:, None], source, 1)
        up_out = lax.dynamic_update_slice_in_dim(up_out, up_k[None], source, 0)
    down_grads = down_out.reshape(2 * half, width)
    up_grads = up_out.reshape(width, 2 * half)

    def halves(x):
        return x[:, :width], x[:, width:]

    block_own, block_send = halves(dot(act, down, (1, 0)))
    token_own, token_send = halves(dot(hid_grads, up, (1, 1)))
    own = jnp.concatenate([block_own, token_own], 1)
    got = swap(jnp.concatenate([block_send, token_send], 1))
    out = (own.astype(f32) + got.astype(f32)).astype(bf16)
    out = exchange(out.reshape(n_row, rows, 2 * width), "row")
    out = jnp.sum(out.astype(f32), 0).astype(bf16)
    return (out[:, :width], out[:, width:], up_grads, down_grads)


def solution(mesh):
    n_row, n_col, n_rep = mesh.devices.shape
    split = Mesh(
        mesh.devices.reshape(n_row, n_col // 2, 2, n_rep), ("row", "z", "core", "rep")
    )
    col = ("z", "core")
    acts = P(("rep", "row"), col)
    up = P(col, "row")
    down = P("row", col)
    return jax.shard_map(
        per_device,
        mesh=split,
        in_specs=(acts, up, down, acts),
        out_specs=(acts, acts, up, down),
        check_vma=False,
    )
```

```python
import jax
import jax.numpy as jnp
from jax import lax
from jax.sharding import Mesh, PartitionSpec as P

bf16 = jnp.bfloat16
f32 = jnp.float32
barrier = lax.optimization_barrier


def gelu_pullback(hidden, upstream):
    _, pullback = jax.vjp(jax.nn.gelu, hidden)
    return pullback(upstream)[0]


def dot(left, right, dims):
    return lax.dot_general(
        left, right, ((dims[:1], dims[1:]), ((), ())), preferred_element_type=f32
    ).astype(bf16)


def swap(x):
    return lax.ppermute(x, "core", [(0, 1), (1, 0)])


def exchange(x, axis):
    return lax.all_to_all(x, axis, 0, 0, tiled=False)


def total_of(x):
    parts = [x[i].astype(f32) for i in range(x.shape[0])]
    while len(parts) > 1:
        parts = [a + b for a, b in zip(parts[::2], parts[1::2])]
    return parts[0]


def gather(x, axis):
    n = lax.axis_size(axis)
    got = exchange(jnp.broadcast_to(x[None], (n,) + x.shape), axis)
    return got.reshape((n * x.shape[0],) + x.shape[1:])


def per_device(tokens, up_weight, down_weight, out_grads):
    core = lax.axis_index("core")
    first = core == 0
    rows, width = tokens.shape
    half = up_weight.shape[1] // 2
    n_row, n_z, n_rep = (lax.axis_size(a) for a in ("row", "z", "rep"))
    mine, theirs = core * half, (1 - core) * half

    def in_order(own, other, axis):
        return jnp.where(
            first,
            jnp.concatenate([own, other], axis),
            jnp.concatenate([other, own], axis),
        )

    up_own = lax.dynamic_slice_in_dim(up_weight, mine, half, 1)
    up_other = swap(lax.dynamic_slice_in_dim(up_weight, theirs, half, 1))
    down_keep = lax.dynamic_slice_in_dim(down_weight, mine, half, 0)
    down_other = swap(lax.dynamic_slice_in_dim(down_weight, theirs, half, 0))
    up = jnp.concatenate([up_own, up_other], 0)
    down = jnp.concatenate([down_keep, down_other], 1)

    tok_own = gather(tokens, "row")
    tok = jnp.concatenate([tok_own, swap(tok_own)], 1)
    total = tok.shape[0]
    share = total // n_z
    hid_part = dot(tok, up, (1, 0)).reshape(n_z, share, half)
    hid_part, out_grads = barrier((hid_part, out_grads))
    hid_terms = exchange(hid_part, "z")
    og_own = lax.all_gather(out_grads, "row", axis=0, tiled=True)
    og = jnp.concatenate([og_own, swap(og_own)], 1)
    ag_part = dot(og, down, (1, 1)).reshape(n_z, share, half)

    hidden = total_of(hid_terms)
    act = jax.nn.gelu(hidden).astype(bf16)
    padded = jnp.pad(act, ((0, share // 2), (0, 0)))
    padded, ag_part = barrier((padded, ag_part))
    act_all = lax.all_gather(padded, "z", axis=0, tiled=False)
    act_all = act_all[:, :share].reshape(total, half)
    act_grads = total_of(exchange(ag_part, "z"))
    hid_grads = gelu_pullback(hidden, act_grads).astype(bf16)
    hg = gather(hid_grads, "z")

    rep = lax.axis_index("rep")
    quarter = half // n_rep

    def shifted(x, k):
        return lax.ppermute(x, "rep", [(i, (i + k) % n_rep) for i in range(n_rep)])

    down_local = dot(act_all, og, (0, 0)).reshape(n_rep, quarter, 2 * width)
    terms = []
    for k in range(n_rep):
        block = lax.dynamic_index_in_dim(down_local, lax.rem(rep + k, n_rep), 0, False)
        terms.append(shifted(block, k) if k else block)
    terms, hg = barrier((terms, hg))
    down_sum = total_of(jnp.stack(terms)).astype(bf16)
    down_own, down_got = down_sum[:, :width], swap(down_sum[:, width:])
    down_pair = in_order(down_own[None], down_got[None], 0)
    down_grads = jnp.zeros((2, n_rep, quarter, width), bf16)
    for k in range(n_rep):
        got = shifted(down_pair, k) if k else down_pair
        source = lax.rem(rep + n_rep - k, n_rep)
        down_grads = lax.dynamic_update_slice_in_dim(down_grads, got[:, None], source, 1)
    down_grads = down_grads.reshape(2 * half, width)

    piece = width // n_rep
    up_local = dot(tok, hg, (0, 0)).reshape(2, n_rep, piece, half)
    up_sum = total_of(exchange(jnp.swapaxes(up_local, 0, 1), "rep")).astype(bf16)
    up_sum = jnp.where(first, up_sum, up_sum[::-1])
    up_send = jnp.broadcast_to(up_sum[:, None], (2, n_rep, piece, half))
    up_all = exchange(up_send.reshape(2 * n_rep, piece, half), ("core", "rep"))
    up_all = up_all.reshape(2, width, half)
    up_grads = jnp.concatenate([up_all[0], up_all[1]], 1)

    def output(left, weight, dims):
        part = dot(left, weight, dims)
        own, other = part[:, :width], swap(part[:, width:])
        return (own.astype(f32) + other.astype(f32)).astype(bf16)

    out = jnp.concatenate([output(act_all, down, (1, 0)), output(hg, up, (1, 1))], 1)
    out = lax.psum_scatter(out, "row", scatter_dimension=0, tiled=True)
    return (out[:, :width], out[:, width:], up_grads, down_grads)


def solution(mesh):
    n_row, n_col, n_rep = mesh.devices.shape
    split = Mesh(
        mesh.devices.reshape(n_row, n_col // 2, 2, n_rep), ("row", "z", "core", "rep")
    )
    col = ("z", "core")
    acts = P(("rep", "row"), col)
    up = P(col, "row")
    down = P("row", col)
    return jax.shard_map(
        per_device,
        mesh=split,
        in_specs=(acts, up, down, acts),
        out_specs=(acts, acts, up, down),
        check_vma=False,
    )
```

```python
import jax
import jax.numpy as jnp
from jax import lax
from jax.sharding import Mesh, PartitionSpec as P

bf16 = jnp.bfloat16
f32 = jnp.float32
barrier = lax.optimization_barrier


def gelu_pullback(hidden, upstream):
    _, pullback = jax.vjp(jax.nn.gelu, hidden)
    return pullback(upstream)[0]


def dot(left, right, dims):
    return lax.dot_general(
        left, right, ((dims[:1], dims[1:]), ((), ())), preferred_element_type=f32
    ).astype(bf16)


def swap(x):
    return lax.ppermute(x, "core", [(0, 1), (1, 0)])


def exchange(x, axis):
    return lax.all_to_all(x, axis, 0, 0, tiled=False)


def total_of(x):
    parts = [x[i].astype(f32) for i in range(x.shape[0])]
    while len(parts) > 1:
        parts = [a + b for a, b in zip(parts[::2], parts[1::2])]
    return parts[0]


def gather(x, axis):
    n = lax.axis_size(axis)
    got = exchange(jnp.broadcast_to(x[None], (n,) + x.shape), axis)
    return got.reshape((n * x.shape[0],) + x.shape[1:])


def per_device(tokens, up_weight, down_weight, out_grads):
    core = lax.axis_index("core")
    first = core == 0
    rows, width = tokens.shape
    half = up_weight.shape[1] // 2
    n_row, n_z, n_rep = (lax.axis_size(a) for a in ("row", "z", "rep"))
    mine, theirs = core * half, (1 - core) * half

    def in_order(own, other, axis):
        return jnp.where(
            first,
            jnp.concatenate([own, other], axis),
            jnp.concatenate([other, own], axis),
        )

    up_own = lax.dynamic_slice_in_dim(up_weight, mine, half, 1)
    up_other = swap(lax.dynamic_slice_in_dim(up_weight, theirs, half, 1))
    down_keep = lax.dynamic_slice_in_dim(down_weight, mine, half, 0)
    down_other = swap(lax.dynamic_slice_in_dim(down_weight, theirs, half, 0))
    up = jnp.concatenate([up_own, up_other], 0)
    down = jnp.concatenate([down_keep, down_other], 1)

    own = gather(jnp.concatenate([tokens, out_grads], 1), "row")
    other = swap(own)
    tok = jnp.concatenate([own[:, :width], other[:, :width]], 1)
    og = jnp.concatenate([own[:, width:], other[:, width:]], 1)
    total = tok.shape[0]
    share = total // n_z
    ag_part = dot(og, down, (1, 1))
    act_grads = lax.psum_scatter(ag_part, "z", scatter_dimension=0, tiled=True)
    hid_part = dot(tok, up, (1, 0)).reshape(n_z, share, half)
    hidden = total_of(exchange(hid_part, "z"))
    act = jax.nn.gelu(hidden).astype(bf16)
    act_all = gather(act, "z")
    act_grads, act_all = barrier((act_grads, act_all))
    hid_grads = gelu_pullback(hidden, act_grads.astype(f32)).astype(bf16)
    hg = gather(hid_grads, "z")

    rep = lax.axis_index("rep")
    quarter = half // n_rep

    def shifted(x, k):
        return lax.ppermute(x, "rep", [(i, (i + k) % n_rep) for i in range(n_rep)])

    down_local = dot(act_all, og, (0, 0)).reshape(n_rep, quarter, 2 * width)
    terms = []
    for k in range(n_rep):
        block = lax.dynamic_index_in_dim(down_local, lax.rem(rep + k, n_rep), 0, False)
        terms.append(shifted(block, k) if k else block)
    down_sum = total_of(jnp.stack(terms)).astype(bf16)
    down_own, down_got = down_sum[:, :width], swap(down_sum[:, width:])
    down_pair = in_order(down_own[None], down_got[None], 0)
    down_grads = jnp.zeros((2, n_rep, quarter, width), bf16)
    for k in range(n_rep):
        got = shifted(down_pair, k) if k else down_pair
        source = lax.rem(rep + n_rep - k, n_rep)
        down_grads = lax.dynamic_update_slice_in_dim(down_grads, got[:, None], source, 1)
    down_grads = down_grads.reshape(2 * half, width)

    piece = width // n_rep
    up_local = dot(tok, hg, (0, 0)).reshape(2, n_rep, piece, half)
    up_sum = total_of(exchange(jnp.swapaxes(up_local, 0, 1), "rep")).astype(bf16)
    up_sum = jnp.where(first, up_sum, up_sum[::-1])
    up_send = jnp.broadcast_to(up_sum[:, None], (2, n_rep, piece, half))
    up_all = exchange(up_send.reshape(2 * n_rep, piece, half), ("core", "rep"))
    up_all = up_all.reshape(2, width, half)
    up_grads = jnp.concatenate([up_all[0], up_all[1]], 1)

    def output(left, weight, dims):
        part = dot(left, weight, dims)
        own, other = part[:, :width], swap(part[:, width:])
        return (own.astype(f32) + other.astype(f32)).astype(bf16)

    out = jnp.concatenate([output(act_all, down, (1, 0)), output(hg, up, (1, 1))], 1)
    out = lax.psum_scatter(out, "row", scatter_dimension=0, tiled=True)
    return (out[:, :width], out[:, width:], up_grads, down_grads)


def solution(mesh):
    n_row, n_col, n_rep = mesh.devices.shape
    split = Mesh(
        mesh.devices.reshape(n_row, n_col // 2, 2, n_rep), ("row", "z", "core", "rep")
    )
    col = ("z", "core")
    acts = P(("rep", "row"), col)
    up = P(col, "row")
    down = P("row", col)
    return jax.shard_map(
        per_device,
        mesh=split,
        in_specs=(acts, up, down, acts),
        out_specs=(acts, acts, up, down),
        check_vma=False,
    )
```

```python
import jax
import jax.numpy as jnp
from jax import lax
from jax.sharding import Mesh, PartitionSpec as P

bf16 = jnp.bfloat16
f32 = jnp.float32
barrier = lax.optimization_barrier


def gelu_pullback(hidden, upstream):
    _, pullback = jax.vjp(jax.nn.gelu, hidden)
    return pullback(upstream)[0]


def dot(left, right, dims):
    return lax.dot_general(
        left, right, ((dims[:1], dims[1:]), ((), ())), preferred_element_type=f32
    ).astype(bf16)


def swap(x):
    return lax.ppermute(x, "core", [(0, 1), (1, 0)])


def exchange(x, axis):
    return lax.all_to_all(x, axis, 0, 0, tiled=False)


def total_of(x):
    parts = [x[i].astype(f32) for i in range(x.shape[0])]
    while len(parts) > 1:
        parts = [a + b for a, b in zip(parts[::2], parts[1::2])]
    return parts[0]


def gather(x, axis):
    n = lax.axis_size(axis)
    got = exchange(jnp.broadcast_to(x[None], (n,) + x.shape), axis)
    return got.reshape((n * x.shape[0],) + x.shape[1:])


def per_device(tokens, up_weight, down_weight, out_grads):
    core = lax.axis_index("core")
    first = core == 0
    rows, width = tokens.shape
    half = up_weight.shape[1] // 2
    n_row, n_z, n_rep = (lax.axis_size(a) for a in ("row", "z", "rep"))
    mine, theirs = core * half, (1 - core) * half

    def in_order(own, other, axis):
        return jnp.where(
            first,
            jnp.concatenate([own, other], axis),
            jnp.concatenate([other, own], axis),
        )

    up_own = lax.dynamic_slice_in_dim(up_weight, mine, half, 1)
    up_other = swap(lax.dynamic_slice_in_dim(up_weight, theirs, half, 1))
    down_keep = lax.dynamic_slice_in_dim(down_weight, mine, half, 0)
    down_other = swap(lax.dynamic_slice_in_dim(down_weight, theirs, half, 0))
    up = jnp.concatenate([up_own, up_other], 0)
    down = jnp.concatenate([down_keep, down_other], 1)

    tok_own = gather(tokens, "row")
    tok = jnp.concatenate([tok_own, swap(tok_own)], 1)
    total = tok.shape[0]
    share = total // n_z
    hid_part = dot(tok, up, (1, 0)).reshape(n_z, share, half)
    hid_part, out_grads = barrier((hid_part, out_grads))
    hid_terms = exchange(hid_part, "z")
    og_own = lax.all_gather(out_grads, "row", axis=0, tiled=True)
    og = jnp.concatenate([og_own, swap(og_own)], 1)
    ag_part = dot(og, down, (1, 1)).reshape(n_z, share, half)

    hidden = total_of(hid_terms)
    act = jax.nn.gelu(hidden).astype(bf16)
    packed = jnp.concatenate(
        [jnp.broadcast_to(act[None], (n_z, share, half)), ag_part], 2
    )
    got = exchange(packed, "z")
    act_all = got[:, :, :half].reshape(total, half)
    act_grads = total_of(got[:, :, half:])
    hid_grads = gelu_pullback(hidden, act_grads).astype(bf16)
    hg = gather(hid_grads, "z")

    rep = lax.axis_index("rep")
    quarter = half // n_rep

    def shifted(x, k):
        return lax.ppermute(x, "rep", [(i, (i + k) % n_rep) for i in range(n_rep)])

    down_local = dot(act_all, og, (0, 0)).reshape(n_rep, quarter, 2 * width)
    terms = []
    for k in range(n_rep):
        block = lax.dynamic_index_in_dim(down_local, lax.rem(rep + k, n_rep), 0, False)
        terms.append(shifted(block, k) if k else block)
    down_sum = total_of(jnp.stack(terms)).astype(bf16)
    down_own, down_got = down_sum[:, :width], swap(down_sum[:, width:])
    down_pair = in_order(down_own[None], down_got[None], 0)
    down_grads = jnp.zeros((2, n_rep, quarter, width), bf16)
    for k in range(n_rep):
        got = shifted(down_pair, k) if k else down_pair
        source = lax.rem(rep + n_rep - k, n_rep)
        down_grads = lax.dynamic_update_slice_in_dim(down_grads, got[:, None], source, 1)
    down_grads = down_grads.reshape(2 * half, width)

    piece = width // n_rep
    up_local = dot(tok, hg, (0, 0)).reshape(2, n_rep, piece, half)
    up_sum = total_of(exchange(jnp.swapaxes(up_local, 0, 1), "rep")).astype(bf16)
    up_sum = jnp.where(first, up_sum, up_sum[::-1])
    up_send = jnp.broadcast_to(up_sum[:, None], (2, n_rep, piece, half))
    up_all = exchange(up_send.reshape(2 * n_rep, piece, half), ("core", "rep"))
    up_all = up_all.reshape(2, width, half)
    up_grads = jnp.concatenate([up_all[0], up_all[1]], 1)

    def output(left, weight, dims):
        part = dot(left, weight, dims)
        own, other = part[:, :width], swap(part[:, width:])
        return (own.astype(f32) + other.astype(f32)).astype(bf16)

    out = jnp.concatenate([output(act_all, down, (1, 0)), output(hg, up, (1, 1))], 1)
    out = out.reshape(n_row, rows, 2 * width)
    row = lax.axis_index("row")
    pieces = []
    for k in range(n_row):
        block = lax.dynamic_index_in_dim(out, lax.rem(row + k, n_row), 0, False)
        ring = [(i, (i + k) % n_row) for i in range(n_row)]
        pieces.append(lax.ppermute(block, "row", ring) if k else block)
    out = total_of(jnp.stack(pieces)).astype(bf16)
    return (out[:, :width], out[:, width:], up_grads, down_grads)


def solution(mesh):
    n_row, n_col, n_rep = mesh.devices.shape
    split = Mesh(
        mesh.devices.reshape(n_row, n_col // 2, 2, n_rep), ("row", "z", "core", "rep")
    )
    col = ("z", "core")
    acts = P(("rep", "row"), col)
    up = P(col, "row")
    down = P("row", col)
    return jax.shard_map(
        per_device,
        mesh=split,
        in_specs=(acts, up, down, acts),
        out_specs=(acts, acts, up, down),
        check_vma=False,
    )
```

```python
import jax
import jax.numpy as jnp
from jax import lax
from jax.sharding import Mesh, PartitionSpec as P

bf16 = jnp.bfloat16
f32 = jnp.float32


def gelu_pullback(hidden, upstream):
    _, pullback = jax.vjp(jax.nn.gelu, hidden)
    return pullback(upstream)[0]


def dot(left, right, dims):
    return lax.dot_general(
        left, right, ((dims[:1], dims[1:]), ((), ())), preferred_element_type=f32
    ).astype(bf16)


def swap(x):
    return lax.ppermute(x, "core", [(0, 1), (1, 0)])


def exchange(x, axis):
    return lax.all_to_all(x, axis, 0, 0, tiled=False)


def total_of(x):
    parts = [x[i].astype(f32) for i in range(x.shape[0])]
    while len(parts) > 1:
        parts = [a + b for a, b in zip(parts[::2], parts[1::2])]
    return parts[0]


def gather(x, axis):
    n = lax.axis_size(axis)
    got = exchange(jnp.broadcast_to(x[None], (n,) + x.shape), axis)
    return got.reshape((n * x.shape[0],) + x.shape[1:])


def pair(own, other, place, axis):
    return jnp.where(
        place == 0,
        jnp.concatenate([own, other], axis),
        jnp.concatenate([other, own], axis),
    )


def per_device(tokens, up_weight, down_weight, out_grads):
    core, zl, rep = (lax.axis_index(a) for a in ("core", "zl", "rep"))
    rows, width = tokens.shape
    half = up_weight.shape[1] // 2
    n_row, n_zh, n_rep = (lax.axis_size(a) for a in ("row", "zh", "rep"))
    n_z = 2 * n_zh
    mine, theirs = core * half, (1 - core) * half

    even = [(p, p ^ 1) for p in range(n_z)]
    odd = [(p, (p + 1 if p % 2 else p - 1) % n_z) for p in range(n_z)]
    near = [(r, r ^ 1) for r in range(n_rep)]
    far = [(r, n_rep - 1 - r) for r in range(n_rep)]

    def z_swap(x, pairs):
        return lax.ppermute(x, ("zh", "zl"), pairs)

    def pick(x, index):
        return lax.dynamic_index_in_dim(x, index, 0, False)

    def plus(a, b):
        return (a.astype(f32) + b.astype(f32)).astype(bf16)

    up_own = lax.dynamic_slice_in_dim(up_weight, mine, half, 1)
    up_other = swap(lax.dynamic_slice_in_dim(up_weight, theirs, half, 1))
    down_own = lax.dynamic_slice_in_dim(down_weight, mine, half, 0)
    down_other = swap(lax.dynamic_slice_in_dim(down_weight, theirs, half, 0))
    up = jnp.concatenate([up_own, up_other], 0)
    down = jnp.concatenate([down_own, down_other], 1)

    own = gather(jnp.concatenate([tokens, out_grads], 1), "row")
    other = swap(own)
    tok = jnp.concatenate([own[:, :width], other[:, :width]], 1)
    og = jnp.concatenate([own[:, width:], other[:, width:]], 1)
    total = tok.shape[0]
    share = total // n_z

    def first_sum(part, pairs):
        part = part.reshape(2, n_zh, share, half)
        return plus(pick(part, zl), z_swap(pick(part, 1 - zl), pairs))

    hid_half = first_sum(dot(tok, up, (1, 0)), even)
    ag_half = first_sum(dot(og, down, (1, 1)), odd)
    sums = total_of(exchange(jnp.concatenate([hid_half, ag_half], 2), "zh"))
    hidden, act_grads = sums[:, :half], sums[:, half:]
    act = jax.nn.gelu(hidden).astype(bf16)
    hid_grads = gelu_pullback(hidden, act_grads).astype(bf16)

    both = lax.all_gather(
        jnp.concatenate([act, hid_grads], 1), "zh", axis=0, tiled=True
    )

    def whole(part, pairs):
        return pair(part, z_swap(part, pairs), zl, 0)

    act, hg = whole(both[:, :half], even), whole(both[:, half:], odd)

    def split(x, bit):
        x = x.reshape((2, x.shape[0] // 2) + x.shape[1:])
        return pick(x, bit), pick(x, 1 - bit)

    def scatter(x, step):
        keep, send = split(x, step[0])
        return plus(keep, lax.ppermute(send, "rep", step[1]))

    def collect(x, steps, axis):
        for bit, pairs in steps[::-1]:
            x = pair(x, lax.ppermute(x, "rep", pairs), bit, axis)
        return x

    high, low = rep // 2, rep % 2
    down_steps = [((rep + 1) // 2 % 2, near), (high, far)]
    up_steps = [(high, far), (low, near)]
    piece = width // n_rep
    down_part = scatter(dot(act, og, (0, 0)), down_steps[0])
    up_part = dot(tok, hg, (0, 0)).reshape(2, n_rep, piece, half)
    up_part = scatter(jnp.swapaxes(up_part, 0, 1), up_steps[0])
    down_part, up_part, act, hg = lax.optimization_barrier(
        (down_part, up_part, act, hg)
    )
    down_part = scatter(down_part, down_steps[1])
    up_part = scatter(up_part, up_steps[1]).reshape(2, piece, half)
    down_part = pair(down_part[None, :, :width], swap(down_part[None, :, width:]), core, 0)
    up_part = pair(up_part[0], swap(up_part[1]), core, 1)
    down_grads = collect(down_part, down_steps, 1).reshape(2 * half, width)
    up_grads = collect(up_part, up_steps, 0)

    def output(left, weight, dims):
        part = dot(left, weight, dims)
        return plus(part[:, :width], swap(part[:, width:]))

    out = jnp.concatenate([output(act, down, (1, 0)), output(hg, up, (1, 1))], 1)
    out = total_of(exchange(out.reshape(n_row, rows, 2 * width), "row")).astype(bf16)
    return (out[:, :width], out[:, width:], up_grads, down_grads)


def solution(mesh):
    n_row, n_col, n_rep = mesh.devices.shape
    split = Mesh(
        mesh.devices.reshape(n_row, n_col // 4, 2, 2, n_rep),
        ("row", "zh", "zl", "core", "rep"),
    )
    col = ("zh", "zl", "core")
    acts = P(("rep", "row"), col)
    up = P(col, "row")
    down = P("row", col)
    return jax.shard_map(
        per_device,
        mesh=split,
        in_specs=(acts, up, down, acts),
        out_specs=(acts, acts, up, down),
        check_vma=False,
    )
```

```python
import jax
import jax.numpy as jnp
from jax import lax
from jax.sharding import Mesh, PartitionSpec as P

bf16 = jnp.bfloat16
f32 = jnp.float32
barrier = lax.optimization_barrier


def gelu_pullback(hidden, upstream):
    _, pullback = jax.vjp(jax.nn.gelu, hidden)
    return pullback(upstream)[0]


def dot(left, right, dims):
    return lax.dot_general(
        left, right, ((dims[:1], dims[1:]), ((), ())), preferred_element_type=f32
    ).astype(bf16)


def swap(x):
    return lax.ppermute(x, "core", [(0, 1), (1, 0)])


def exchange(x, axis):
    return lax.all_to_all(x, axis, 0, 0, tiled=False)


def total_of(x):
    parts = [x[i].astype(f32) for i in range(x.shape[0])]
    while len(parts) > 1:
        parts = [a + b for a, b in zip(parts[::2], parts[1::2])]
    return parts[0]


def gather(x, axis):
    n = lax.axis_size(axis)
    got = exchange(jnp.broadcast_to(x[None], (n,) + x.shape), axis)
    return got.reshape((n * x.shape[0],) + x.shape[1:])


def pair(own, other, place, axis):
    return jnp.where(
        place == 0,
        jnp.concatenate([own, other], axis),
        jnp.concatenate([other, own], axis),
    )


def per_device(tokens, up_weight, down_weight, out_grads):
    core, zl, rep = (lax.axis_index(a) for a in ("core", "zl", "rep"))
    rows, width = tokens.shape
    half = up_weight.shape[1] // 2
    n_row, n_zh, n_rep = (lax.axis_size(a) for a in ("row", "zh", "rep"))
    n_z = 2 * n_zh
    mine, theirs = core * half, (1 - core) * half

    even = [(p, p ^ 1) for p in range(n_z)]
    odd = [(p, (p + 1 if p % 2 else p - 1) % n_z) for p in range(n_z)]
    near = [(r, r ^ 1) for r in range(n_rep)]
    far = [(r, n_rep - 1 - r) for r in range(n_rep)]

    def z_swap(x, pairs):
        return lax.ppermute(x, ("zh", "zl"), pairs)

    def pick(x, index):
        return lax.dynamic_index_in_dim(x, index, 0, False)

    def plus(a, b):
        return (a.astype(f32) + b.astype(f32)).astype(bf16)

    up_keep = lax.dynamic_slice_in_dim(up_weight, mine, half, 1)
    up_other = swap(lax.dynamic_slice_in_dim(up_weight, theirs, half, 1))
    down_keep = lax.dynamic_slice_in_dim(down_weight, mine, half, 0)
    down_other = swap(lax.dynamic_slice_in_dim(down_weight, theirs, half, 0))
    up = jnp.concatenate([up_keep, up_other], 0)
    down = jnp.concatenate([down_keep, down_other], 1)

    own = gather(jnp.concatenate([tokens, out_grads], 1), "row")
    own, up, down = barrier((own, up, down))
    other = swap(own)
    tok = jnp.concatenate([own[:, :width], other[:, :width]], 1)
    og = jnp.concatenate([own[:, width:], other[:, width:]], 1)
    total = tok.shape[0]
    share = total // n_z

    def halves(part):
        part = part.reshape(2, n_zh, share, half)
        return pick(part, zl), pick(part, 1 - zl)

    hid_keep, hid_send = halves(dot(tok, up, (1, 0)))
    ag_keep, ag_send = halves(dot(og, down, (1, 1)))
    hid_send, ag_send = barrier((hid_send, ag_send))
    hid_half = plus(hid_keep, z_swap(hid_send, even))
    ag_half = plus(ag_keep, z_swap(ag_send, odd))
    sums = total_of(exchange(jnp.concatenate([hid_half, ag_half], 2), "zh"))
    hidden, act_grads = sums[:, :half], sums[:, half:]
    act = jax.nn.gelu(hidden).astype(bf16)
    hid_grads = gelu_pullback(hidden, act_grads).astype(bf16)

    both = lax.all_gather(
        jnp.concatenate([act, hid_grads], 1), "zh", axis=0, tiled=True
    )

    def whole(part, pairs):
        return pair(part, z_swap(part, pairs), zl, 0)

    act, hg = whole(both[:, :half], even), whole(both[:, half:], odd)

    def scatter(keep, send, step):
        return plus(keep, lax.ppermute(send, "rep", step[1]))

    def collect(x, steps, axis):
        for bit, pairs in steps[::-1]:
            x = pair(x, lax.ppermute(x, "rep", pairs), bit, axis)
        return x

    def parts(own, got, bit, axis):
        own, got = (x.reshape((2, x.shape[0] // 2) + x.shape[1:]) for x in (own, got))
        return tuple(
            pair(pick(own, b)[None], pick(got, b)[None], core, 0)
            if axis == 0
            else pair(pick(own, b), pick(got, b), core, 1)
            for b in (bit, 1 - bit)
        )

    high, low = rep // 2, rep % 2
    down_steps = [((rep + 1) // 2 % 2, near), (high, far)]
    up_steps = [(high, far), (low, near)]
    down_got = swap(dot(act, og[:, width:], (0, 0)))
    up_got = swap(dot(tok[:, width:], hg, (0, 0)))
    down_own = dot(act, og[:, :width], (0, 0))
    up_own = dot(tok[:, :width], hg, (0, 0))
    down_part = scatter(*parts(down_own, down_got, down_steps[0][0], 0), down_steps[0])
    up_part = scatter(*parts(up_own, up_got, up_steps[0][0], 1), up_steps[0])
    down_part, act, hg = barrier((down_part, act, hg))
    down_part = down_part.reshape(2, 2, -1, width)
    bit = down_steps[1][0]
    down_part = scatter(
        lax.dynamic_index_in_dim(down_part, bit, 1, False),
        lax.dynamic_index_in_dim(down_part, 1 - bit, 1, False),
        down_steps[1],
    )
    up_part = up_part.reshape(2, -1, 2 * half)
    bit = up_steps[1][0]
    up_part = scatter(pick(up_part, bit), pick(up_part, 1 - bit), up_steps[1])
    down_grads = collect(down_part, down_steps, 1).reshape(2 * half, width)
    up_grads = collect(up_part, up_steps, 0)

    block, token = dot(act, down, (1, 0)), dot(hg, up, (1, 1))
    out = plus(
        jnp.concatenate([block[:, :width], token[:, :width]], 1),
        swap(jnp.concatenate([block[:, width:], token[:, width:]], 1)),
    )
    out = total_of(exchange(out.reshape(n_row, rows, 2 * width), "row")).astype(bf16)
    return (out[:, :width], out[:, width:], up_grads, down_grads)


def solution(mesh):
    n_row, n_col, n_rep = mesh.devices.shape
    split = Mesh(
        mesh.devices.reshape(n_row, n_col // 4, 2, 2, n_rep),
        ("row", "zh", "zl", "core", "rep"),
    )
    col = ("zh", "zl", "core")
    acts = P(("rep", "row"), col)
    up = P(col, "row")
    down = P("row", col)
    return jax.shard_map(
        per_device,
        mesh=split,
        in_specs=(acts, up, down, acts),
        out_specs=(acts, acts, up, down),
        check_vma=False,
    )
```

```python
import jax
import jax.numpy as jnp
from jax import lax
from jax.sharding import Mesh, PartitionSpec as P

bf16 = jnp.bfloat16
f32 = jnp.float32
barrier = lax.optimization_barrier


def gelu_pullback(hidden, upstream):
    _, pullback = jax.vjp(jax.nn.gelu, hidden)
    return pullback(upstream)[0]


def dot(left, right, dims):
    return lax.dot_general(
        left, right, ((dims[:1], dims[1:]), ((), ())), preferred_element_type=f32
    ).astype(bf16)


def swap(x):
    return lax.ppermute(x, "core", [(0, 1), (1, 0)])


def exchange(x, axis):
    return lax.all_to_all(x, axis, 0, 0, tiled=False)


def total_of(x):
    parts = [x[i].astype(f32) for i in range(x.shape[0])]
    while len(parts) > 1:
        parts = [a + b for a, b in zip(parts[::2], parts[1::2])]
    return parts[0]


def gather(x, axis):
    n = lax.axis_size(axis)
    got = exchange(jnp.broadcast_to(x[None], (n,) + x.shape), axis)
    return got.reshape((n * x.shape[0],) + x.shape[1:])


def pair(own, other, place, axis):
    return jnp.where(
        place == 0,
        jnp.concatenate([own, other], axis),
        jnp.concatenate([other, own], axis),
    )


def per_device(tokens, up_weight, down_weight, out_grads):
    core, zl, rep = (lax.axis_index(a) for a in ("core", "zl", "rep"))
    rows, width = tokens.shape
    half = up_weight.shape[1] // 2
    n_row, n_zh, n_rep = (lax.axis_size(a) for a in ("row", "zh", "rep"))
    n_z = 2 * n_zh
    mine, theirs = core * half, (1 - core) * half

    even = [(p, p ^ 1) for p in range(n_z)]
    odd = [(p, (p + 1 if p % 2 else p - 1) % n_z) for p in range(n_z)]
    near = [(r, r ^ 1) for r in range(n_rep)]
    far = [(r, n_rep - 1 - r) for r in range(n_rep)]

    def z_swap(x, pairs):
        return lax.ppermute(x, ("zh", "zl"), pairs)

    def pick(x, index):
        return lax.dynamic_index_in_dim(x, index, 0, False)

    def plus(a, b):
        return (a.astype(f32) + b.astype(f32)).astype(bf16)

    up_keep = lax.dynamic_slice_in_dim(up_weight, mine, half, 1)
    up_other = swap(lax.dynamic_slice_in_dim(up_weight, theirs, half, 1))
    down_keep = lax.dynamic_slice_in_dim(down_weight, mine, half, 0)
    down_other = swap(lax.dynamic_slice_in_dim(down_weight, theirs, half, 0))
    up = jnp.concatenate([up_keep, up_other], 0)
    down = jnp.concatenate([down_keep, down_other], 1)

    own = gather(jnp.concatenate([tokens, out_grads], 1), "row")
    own, up, down = barrier((own, up, down))
    other = swap(own)
    tok = jnp.concatenate([own[:, :width], other[:, :width]], 1)
    og = jnp.concatenate([own[:, width:], other[:, width:]], 1)
    total = tok.shape[0]
    share = total // n_z

    def halves(part):
        part = part.reshape(2, n_zh, share, half)
        return pick(part, zl), pick(part, 1 - zl)

    hid_keep, hid_send = halves(dot(tok, up, (1, 0)))
    ag_keep, ag_send = halves(dot(og, down, (1, 1)))
    hid_send, ag_send = barrier((hid_send, ag_send))
    hid_half = plus(hid_keep, z_swap(hid_send, even))
    ag_half = plus(ag_keep, z_swap(ag_send, odd))
    sums = total_of(exchange(jnp.concatenate([hid_half, ag_half], 2), "zh"))
    hidden, act_grads = sums[:, :half], sums[:, half:]
    act = jax.nn.gelu(hidden).astype(bf16)
    hid_grads = gelu_pullback(hidden, act_grads).astype(bf16)

    act_half = lax.all_gather(act, "zh", axis=0, tiled=True)
    act_half, hid_grads = barrier((act_half, hid_grads))
    hg_half = gather(hid_grads, "zh")
    act = pair(act_half, z_swap(act_half, even), zl, 0)
    hg = pair(hg_half, z_swap(hg_half, odd), zl, 0)

    near_bit, far_bit = (rep + 1) // 2 % 2, rep // 2
    down_got = swap(dot(act, og[:, width:], (0, 0)))
    down_own = dot(act, og[:, :width], (0, 0))
    own_got = [x.reshape(2, half // 2, width) for x in (down_own, down_got)]

    def chosen(bit):
        return pair(*(pick(x, bit)[None] for x in own_got), core, 0)

    down_part = plus(chosen(near_bit), lax.ppermute(chosen(1 - near_bit), "rep", near))
    down_part = jnp.swapaxes(down_part.reshape(2, 2, -1, width), 0, 1)
    send, block_act, token_hg = barrier((pick(down_part, 1 - far_bit), act, hg))
    down_part = plus(pick(down_part, far_bit), lax.ppermute(send, "rep", far))
    down_part = pair(down_part, lax.ppermute(down_part, "rep", far), far_bit, 1)
    down_part = pair(down_part, lax.ppermute(down_part, "rep", near), near_bit, 1)
    down_grads = down_part.reshape(2 * half, width)

    piece = width // n_rep
    up_part = dot(tok, hg, (0, 0)).reshape(2, n_rep, piece, half)
    up_part = total_of(exchange(jnp.swapaxes(up_part, 0, 1), "rep")).astype(bf16)
    block, token = dot(block_act, down, (1, 0)), dot(token_hg, up, (1, 1))
    out = plus(
        jnp.concatenate([block[:, :width], token[:, :width]], 1),
        swap(jnp.concatenate([block[:, width:], token[:, width:]], 1)),
    )
    up_part, out = barrier((up_part, out))
    out = total_of(exchange(out.reshape(n_row, rows, 2 * width), "row")).astype(bf16)
    up_part = pair(up_part[0], swap(up_part[1]), core, 1)
    up_grads = jnp.zeros((n_rep, piece, 2 * half), bf16)
    for k in range(n_rep):
        ring = [(i, (i + k) % n_rep) for i in range(n_rep)]
        got = lax.ppermute(up_part, "rep", ring) if k else up_part
        source = lax.rem(rep + n_rep - k, n_rep)
        up_grads = lax.dynamic_update_slice_in_dim(up_grads, got[None], source, 0)
    up_grads = up_grads.reshape(width, 2 * half)

    return (out[:, :width], out[:, width:], up_grads, down_grads)


def solution(mesh):
    n_row, n_col, n_rep = mesh.devices.shape
    split = Mesh(
        mesh.devices.reshape(n_row, n_col // 4, 2, 2, n_rep),
        ("row", "zh", "zl", "core", "rep"),
    )
    col = ("zh", "zl", "core")
    acts = P(("rep", "row"), col)
    up = P(col, "row")
    down = P("row", col)
    return jax.shard_map(
        per_device,
        mesh=split,
        in_specs=(acts, up, down, acts),
        out_specs=(acts, acts, up, down),
        check_vma=False,
    )
```

```python
import jax
import jax.numpy as jnp
from jax import lax
from jax.sharding import Mesh, PartitionSpec as P

bf16 = jnp.bfloat16
f32 = jnp.float32
barrier = lax.optimization_barrier


def gelu_pullback(hidden, upstream):
    _, pullback = jax.vjp(jax.nn.gelu, hidden)
    return pullback(upstream)[0]


def dot(left, right, dims):
    return lax.dot_general(
        left, right, ((dims[:1], dims[1:]), ((), ())), preferred_element_type=f32
    ).astype(bf16)


def swap(x):
    return lax.ppermute(x, "core", [(0, 1), (1, 0)])


def exchange(x, axis):
    return lax.all_to_all(x, axis, 0, 0, tiled=False)


def total_of(x):
    parts = [x[i].astype(f32) for i in range(x.shape[0])]
    while len(parts) > 1:
        parts = [a + b for a, b in zip(parts[::2], parts[1::2])]
    return parts[0]


def gather(x, axis):
    n = lax.axis_size(axis)
    got = exchange(jnp.broadcast_to(x[None], (n,) + x.shape), axis)
    return got.reshape((n * x.shape[0],) + x.shape[1:])


def pair(own, other, place, axis):
    return jnp.where(
        place == 0,
        jnp.concatenate([own, other], axis),
        jnp.concatenate([other, own], axis),
    )


def per_device(tokens, up_weight, down_weight, out_grads):
    core, zl, rep = (lax.axis_index(a) for a in ("core", "zl", "rep"))
    rows, width = tokens.shape
    half = up_weight.shape[1] // 2
    n_row, n_zh, n_rep = (lax.axis_size(a) for a in ("row", "zh", "rep"))
    n_z = 2 * n_zh
    mine, theirs = core * half, (1 - core) * half

    even = [(p, p ^ 1) for p in range(n_z)]
    odd = [(p, (p + 1 if p % 2 else p - 1) % n_z) for p in range(n_z)]
    near = [(r, r ^ 1) for r in range(n_rep)]
    far = [(r, n_rep - 1 - r) for r in range(n_rep)]

    def z_swap(x, pairs):
        return lax.ppermute(x, ("zh", "zl"), pairs)

    def pick(x, index):
        return lax.dynamic_index_in_dim(x, index, 0, False)

    def plus(a, b):
        return (a.astype(f32) + b.astype(f32)).astype(bf16)

    up_keep = lax.dynamic_slice_in_dim(up_weight, mine, half, 1)
    up_other = swap(lax.dynamic_slice_in_dim(up_weight, theirs, half, 1))
    down_keep = lax.dynamic_slice_in_dim(down_weight, mine, half, 0)
    down_other = swap(lax.dynamic_slice_in_dim(down_weight, theirs, half, 0))
    up = jnp.concatenate([up_keep, up_other], 0)
    down = jnp.concatenate([down_keep, down_other], 1)

    own = gather(jnp.concatenate([tokens, out_grads], 1), "row")
    own, up, down = barrier((own, up, down))
    other = swap(own)
    tok = jnp.concatenate([own[:, :width], other[:, :width]], 1)
    og = jnp.concatenate([own[:, width:], other[:, width:]], 1)
    total = tok.shape[0]
    share = total // n_z

    def halves(part):
        part = part.reshape(2, n_zh, share, half)
        return pick(part, zl), pick(part, 1 - zl)

    hid_keep, hid_send = halves(dot(tok, up, (1, 0)))
    ag_keep, ag_send = halves(dot(og, down, (1, 1)))
    hid_send, ag_send = barrier((hid_send, ag_send))
    hid_half = plus(hid_keep, z_swap(hid_send, even))
    ag_half = plus(ag_keep, z_swap(ag_send, odd))
    sums = total_of(exchange(jnp.concatenate([hid_half, ag_half], 2), "zh"))
    hidden, act_grads = sums[:, :half], sums[:, half:]
    act = jax.nn.gelu(hidden).astype(bf16)
    hid_grads = gelu_pullback(hidden, act_grads).astype(bf16)

    both = lax.all_gather(
        jnp.concatenate([act, hid_grads], 1), "zh", axis=0, tiled=True
    )

    def whole(part, pairs):
        return pair(part, z_swap(part, pairs), zl, 0)

    act, hg = whole(both[:, :half], even), whole(both[:, half:], odd)

    def scatter(x, axis, bit, pairs):
        def at(place):
            return lax.dynamic_index_in_dim(x, place, axis, False)

        return plus(at(bit), lax.ppermute(at(1 - bit), "rep", pairs))

    def collect(x, steps, axis):
        for bit, pairs in steps:
            x = pair(x, lax.ppermute(x, "rep", pairs), bit, axis)
        return x

    turn, high, low = (rep + 1) // 2 % 2, rep // 2, rep % 2
    down_part = dot(act, og, (0, 0)).reshape(2, 2, -1, 2 * width)
    down_part = scatter(down_part, 0, turn, near)
    up_part = dot(tok, hg, (0, 0)).reshape(2, 2, 2, -1, half)
    up_part = scatter(up_part, 1, high, far)
    down_part = scatter(down_part, 0, high, far)
    down_part, act, hg = barrier((down_part, act, hg))
    up_part = scatter(up_part, 1, low, near)
    down_own, down_got = down_part[:, :width], swap(down_part[:, width:])
    down_part = pair(down_own[None], down_got[None], core, 0)
    down_part = collect(down_part, [(high, far), (turn, near)], 1)
    down_grads = down_part.reshape(2 * half, width)
    up_part = pair(up_part[0], swap(up_part[1]), core, 1)
    up_grads = collect(up_part, [(low, near), (high, far)], 0)

    block, token = dot(act, down, (1, 0)), dot(hg, up, (1, 1))
    out = plus(
        jnp.concatenate([block[:, :width], token[:, :width]], 1),
        swap(jnp.concatenate([block[:, width:], token[:, width:]], 1)),
    )
    out = total_of(exchange(out.reshape(n_row, rows, 2 * width), "row")).astype(bf16)
    return (out[:, :width], out[:, width:], up_grads, down_grads)


def solution(mesh):
    n_row, n_col, n_rep = mesh.devices.shape
    split = Mesh(
        mesh.devices.reshape(n_row, n_col // 4, 2, 2, n_rep),
        ("row", "zh", "zl", "core", "rep"),
    )
    col = ("zh", "zl", "core")
    acts = P(("rep", "row"), col)
    up = P(col, "row")
    down = P("row", col)
    return jax.shard_map(
        per_device,
        mesh=split,
        in_specs=(acts, up, down, acts),
        out_specs=(acts, acts, up, down),
        check_vma=False,
    )
```

```python
import jax
import jax.numpy as jnp
from jax import lax
from jax.sharding import Mesh, PartitionSpec as P

bf16 = jnp.bfloat16
f32 = jnp.float32
barrier = lax.optimization_barrier


def gelu_pullback(hidden, upstream):
    _, pullback = jax.vjp(jax.nn.gelu, hidden)
    return pullback(upstream)[0]


def dot(left, right, dims):
    return lax.dot_general(
        left, right, ((dims[:1], dims[1:]), ((), ())), preferred_element_type=f32
    ).astype(bf16)


def swap(x):
    return lax.ppermute(x, "core", [(0, 1), (1, 0)])


def exchange(x, axis):
    return lax.all_to_all(x, axis, 0, 0, tiled=False)


def total_of(x):
    parts = [x[i].astype(f32) for i in range(x.shape[0])]
    while len(parts) > 1:
        parts = [a + b for a, b in zip(parts[::2], parts[1::2])]
    return parts[0]


def gather(x, axis):
    n = lax.axis_size(axis)
    got = exchange(jnp.broadcast_to(x[None], (n,) + x.shape), axis)
    return got.reshape((n * x.shape[0],) + x.shape[1:])


def pair(own, other, place, axis):
    return jnp.where(
        place == 0,
        jnp.concatenate([own, other], axis),
        jnp.concatenate([other, own], axis),
    )


def per_device(tokens, up_weight, down_weight, out_grads):
    core, zl, rep = (lax.axis_index(a) for a in ("core", "zl", "rep"))
    rows, width = tokens.shape
    half = up_weight.shape[1] // 2
    n_row, n_zh, n_rep = (lax.axis_size(a) for a in ("row", "zh", "rep"))
    n_z = 2 * n_zh
    mine, theirs = core * half, (1 - core) * half

    even = [(p, p ^ 1) for p in range(n_z)]
    odd = [(p, (p + 1 if p % 2 else p - 1) % n_z) for p in range(n_z)]
    near = [(r, r ^ 1) for r in range(n_rep)]
    far = [(r, n_rep - 1 - r) for r in range(n_rep)]

    def z_swap(x, pairs):
        return lax.ppermute(x, ("zh", "zl"), pairs)

    def pick(x, index):
        return lax.dynamic_index_in_dim(x, index, 0, False)

    def plus(a, b):
        return (a.astype(f32) + b.astype(f32)).astype(bf16)

    up_keep = lax.dynamic_slice_in_dim(up_weight, mine, half, 1)
    up_other = swap(lax.dynamic_slice_in_dim(up_weight, theirs, half, 1))
    down_keep = lax.dynamic_slice_in_dim(down_weight, mine, half, 0)
    down_other = swap(lax.dynamic_slice_in_dim(down_weight, theirs, half, 0))
    up = jnp.concatenate([up_keep, up_other], 0)
    down = jnp.concatenate([down_keep, down_other], 1)

    own = gather(jnp.concatenate([tokens, out_grads], 1), "row")
    own, up, down = barrier((own, up, down))
    other = swap(own)
    total = own.shape[0]
    same, share = total // 2, total // n_z

    def columns_of(x, place):
        x = pick(x.reshape(2, same, 2 * width), place)
        return x[:, :width], x[:, width:]

    def rows_of(place):
        (t0, g0), (t1, g1) = columns_of(own, place), columns_of(other, place)
        return jnp.concatenate([t0, t1], 1), jnp.concatenate([g0, g1], 1)

    tok_send, og_send = rows_of(1 - zl)
    tok_keep, og_keep = rows_of(zl)

    hid_send = dot(tok_send, up, (1, 0))
    ag_send = dot(og_send, down, (1, 1))
    hid_send, ag_send, tok_keep, og_keep = barrier(
        (hid_send, ag_send, tok_keep, og_keep)
    )
    tok = jnp.concatenate([tok_keep, tok_send], 0)
    og = jnp.concatenate([og_keep, og_send], 0)
    hid_half = plus(dot(tok_keep, up, (1, 0)), z_swap(hid_send, even))
    ag_half = plus(dot(og_keep, down, (1, 1)), z_swap(ag_send, odd))
    halves = jnp.concatenate([hid_half, ag_half], 1).reshape(n_zh, share, 2 * half)
    sums = total_of(exchange(halves, "zh"))
    hidden, act_grads = sums[:, :half], sums[:, half:]
    act = jax.nn.gelu(hidden).astype(bf16)
    hid_grads = gelu_pullback(hidden, act_grads).astype(bf16)

    both = lax.all_gather(
        jnp.concatenate([act, hid_grads], 1), "zh", axis=0, tiled=True
    )

    act_half, hg_half = both[:, :half], both[:, half:]
    act_got, hg_got = z_swap(act_half, even), z_swap(hg_half, odd)
    act = jnp.concatenate([act_half, act_got], 0)
    hg = jnp.concatenate([hg_half, hg_got], 0)

    def scatter(x, axis, bit, pairs):
        def at(place):
            return lax.dynamic_index_in_dim(x, place, axis, False)

        return plus(at(bit), lax.ppermute(at(1 - bit), "rep", pairs))

    def collect(x, steps, axis):
        for bit, pairs in steps:
            x = pair(x, lax.ppermute(x, "rep", pairs), bit, axis)
        return x

    turn, high, low = (rep + 1) // 2 % 2, rep // 2, rep % 2
    down_part = dot(act, og, (0, 0)).reshape(2, 2, -1, 2 * width)
    down_part = scatter(down_part, 0, turn, near)
    cut = width // 2
    order = [tok[:, i * cut : (i + 1) * cut] for i in (0, 2, 1, 3)]
    up_part = dot(jnp.concatenate(order, 1), hg, (0, 0)).reshape(2, width, half)
    up_part = scatter(up_part, 0, high, far).reshape(2, 2, -1, half)
    down_part = scatter(down_part, 0, high, far)
    down_part, act_half, act_got, hg_half, hg_got = barrier(
        (down_part, act_half, act_got, hg_half, hg_got)
    )
    up_part = scatter(up_part, 1, low, near)
    down_own, down_got = down_part[:, :width], swap(down_part[:, width:])
    down_part = pair(down_own[None], down_got[None], core, 0)
    down_part = collect(down_part, [(high, far), (turn, near)], 1)
    down_grads = down_part.reshape(2 * half, width)
    up_part = pair(up_part[0], swap(up_part[1]), core, 1)
    up_grads = collect(up_part, [(low, near), (high, far)], 0)

    act, hg = pair(act_half, act_got, zl, 0), pair(hg_half, hg_got, zl, 0)

    def output(columns):
        block = dot(act, down[:, columns], (1, 0))
        token = dot(hg, up[columns], (1, 1))
        return jnp.concatenate([block, token], 1)

    send = output(slice(width, None))
    out = plus(output(slice(width)), swap(send))
    out = total_of(exchange(out.reshape(n_row, rows, 2 * width), "row")).astype(bf16)
    return (out[:, :width], out[:, width:], up_grads, down_grads)


def solution(mesh):
    n_row, n_col, n_rep = mesh.devices.shape
    split = Mesh(
        mesh.devices.reshape(n_row, n_col // 4, 2, 2, n_rep),
        ("row", "zh", "zl", "core", "rep"),
    )
    col = ("zh", "zl", "core")
    acts = P(("rep", "row"), col)
    up = P(col, "row")
    down = P("row", col)
    return jax.shard_map(
        per_device,
        mesh=split,
        in_specs=(acts, up, down, acts),
        out_specs=(acts, acts, up, down),
        check_vma=False,
    )
```

```python
import jax
import jax.numpy as jnp
from jax import lax
from jax.sharding import Mesh, PartitionSpec as P

bf16 = jnp.bfloat16
f32 = jnp.float32
barrier = lax.optimization_barrier


def gelu_pullback(hidden, upstream):
    _, pullback = jax.vjp(jax.nn.gelu, hidden)
    return pullback(upstream)[0]


def dot(left, right, dims):
    return lax.dot_general(
        left, right, ((dims[:1], dims[1:]), ((), ())), preferred_element_type=f32
    ).astype(bf16)


def swap(x):
    return lax.ppermute(x, "core", [(0, 1), (1, 0)])


def exchange(x, axis):
    return lax.all_to_all(x, axis, 0, 0, tiled=False)


def total_of(x):
    parts = [x[i].astype(f32) for i in range(x.shape[0])]
    while len(parts) > 1:
        parts = [a + b for a, b in zip(parts[::2], parts[1::2])]
    return parts[0]


def gather(x, axis):
    n = lax.axis_size(axis)
    got = exchange(jnp.broadcast_to(x[None], (n,) + x.shape), axis)
    return got.reshape((n * x.shape[0],) + x.shape[1:])


def pair(own, other, place, axis):
    return jnp.where(
        place == 0,
        jnp.concatenate([own, other], axis),
        jnp.concatenate([other, own], axis),
    )


def per_device(tokens, up_weight, down_weight, out_grads):
    core, zl, rep = (lax.axis_index(a) for a in ("core", "zl", "rep"))
    rows, width = tokens.shape
    half = up_weight.shape[1] // 2
    n_row, n_zh, n_rep = (lax.axis_size(a) for a in ("row", "zh", "rep"))
    n_z = 2 * n_zh
    mine, theirs = core * half, (1 - core) * half

    even = [(p, p ^ 1) for p in range(n_z)]
    odd = [(p, (p + 1 if p % 2 else p - 1) % n_z) for p in range(n_z)]
    near = [(r, r ^ 1) for r in range(n_rep)]
    far = [(r, n_rep - 1 - r) for r in range(n_rep)]

    def z_swap(x, pairs):
        return lax.ppermute(x, ("zh", "zl"), pairs)

    def pick(x, index):
        return lax.dynamic_index_in_dim(x, index, 0, False)

    def plus(a, b):
        return (a.astype(f32) + b.astype(f32)).astype(bf16)

    up_keep = lax.dynamic_slice_in_dim(up_weight, mine, half, 1)
    up_other = swap(lax.dynamic_slice_in_dim(up_weight, theirs, half, 1))
    down_keep = lax.dynamic_slice_in_dim(down_weight, mine, half, 0)
    down_other = swap(lax.dynamic_slice_in_dim(down_weight, theirs, half, 0))
    up = jnp.concatenate([up_keep, up_other], 0)
    down = jnp.concatenate([down_keep, down_other], 1)

    own = gather(jnp.concatenate([tokens, out_grads], 1), "row")
    own, up, down = barrier((own, up, down))
    other = swap(own)
    total = own.shape[0]
    same, share = total // 2, total // n_z

    def columns_of(x, place):
        x = pick(x.reshape(2, same, 2 * width), place)
        return x[:, :width], x[:, width:]

    def rows_of(place):
        (t0, g0), (t1, g1) = columns_of(own, place), columns_of(other, place)
        return jnp.concatenate([t0, t1], 1), jnp.concatenate([g0, g1], 1)

    tok_send, og_send = rows_of(1 - zl)
    tok_keep, og_keep = rows_of(zl)

    hid_send = dot(tok_send, up, (1, 0))
    ag_send = dot(og_send, down, (1, 1))
    hid_send, ag_send, tok_keep, og_keep = barrier(
        (hid_send, ag_send, tok_keep, og_keep)
    )
    tok = jnp.concatenate([tok_keep, tok_send], 0)
    og = jnp.concatenate([og_keep, og_send], 0)
    hid_half = plus(dot(tok_keep, up, (1, 0)), z_swap(hid_send, even))
    ag_half = plus(dot(og_keep, down, (1, 1)), z_swap(ag_send, odd))
    halves = jnp.concatenate([hid_half, ag_half], 1).reshape(n_zh, share, 2 * half)
    sums = total_of(exchange(halves, "zh"))
    hidden, act_grads = sums[:, :half], sums[:, half:]
    act = jax.nn.gelu(hidden).astype(bf16)
    hid_grads = gelu_pullback(hidden, act_grads).astype(bf16)

    both = lax.all_gather(
        jnp.concatenate([act, hid_grads], 1), "zh", axis=0, tiled=True
    )

    act_half, hg_half = both[:, :half], both[:, half:]
    act_got, hg_got = z_swap(act_half, even), z_swap(hg_half, odd)
    act = jnp.concatenate([act_half, act_got], 0)
    hg = jnp.concatenate([hg_half, hg_got], 0)

    def scatter(x, axis, bit, pairs):
        def at(place):
            return lax.dynamic_index_in_dim(x, place, axis, False)

        return plus(at(bit), lax.ppermute(at(1 - bit), "rep", pairs))

    turn, high = (rep + 1) // 2 % 2, rep // 2
    down_part = dot(act, og, (0, 0)).reshape(2, half // 2, 2 * width)
    down_part = scatter(down_part, 0, turn, near)
    down_part, act_half, act_got, hg_half, hg_got = barrier(
        (down_part, act_half, act_got, hg_half, hg_got)
    )
    cut = width // 2
    order = [tok[:, i * cut : (i + 1) * cut] for i in (0, 2, 1, 3)]
    up_part = dot(jnp.concatenate(order, 1), hg, (0, 0)).reshape(2, width, half)
    up_part = scatter(up_part, 0, high, far)
    down_part = plus(down_part, lax.ppermute(down_part, "rep", far))
    up_part = plus(up_part, lax.ppermute(up_part, "rep", near))
    down_own, down_got = down_part[:, :width], swap(down_part[:, width:])
    down_part = pair(down_own[None], down_got[None], core, 0)
    down_part = pair(down_part, lax.ppermute(down_part, "rep", near), turn, 1)
    down_grads = down_part.reshape(2 * half, width)
    up_part = pair(up_part[:cut], swap(up_part[cut:]), core, 1)
    up_grads = pair(up_part, lax.ppermute(up_part, "rep", far), high, 0)

    act, hg = pair(act_half, act_got, zl, 0), pair(hg_half, hg_got, zl, 0)

    def output(columns):
        block = dot(act, down[:, columns], (1, 0))
        token = dot(hg, up[columns], (1, 1))
        return jnp.concatenate([block, token], 1)

    send = output(slice(width, None))
    out = plus(output(slice(width)), swap(send))
    out = total_of(exchange(out.reshape(n_row, rows, 2 * width), "row")).astype(bf16)
    return (out[:, :width], out[:, width:], up_grads, down_grads)


def solution(mesh):
    n_row, n_col, n_rep = mesh.devices.shape
    split = Mesh(
        mesh.devices.reshape(n_row, n_col // 4, 2, 2, n_rep),
        ("row", "zh", "zl", "core", "rep"),
    )
    col = ("zh", "zl", "core")
    acts = P(("rep", "row"), col)
    up = P(col, "row")
    down = P("row", col)
    return jax.shard_map(
        per_device,
        mesh=split,
        in_specs=(acts, up, down, acts),
        out_specs=(acts, acts, up, down),
        check_vma=False,
    )
```

```python
import jax
import jax.numpy as jnp
from jax import lax
from jax.sharding import Mesh, PartitionSpec as P

bf16 = jnp.bfloat16
f32 = jnp.float32
barrier = lax.optimization_barrier


def gelu_pullback(hidden, upstream):
    _, pullback = jax.vjp(jax.nn.gelu, hidden)
    return pullback(upstream)[0]


def dot(left, right, dims):
    return lax.dot_general(
        left, right, ((dims[:1], dims[1:]), ((), ())), preferred_element_type=f32
    ).astype(bf16)


def swap(x):
    return lax.ppermute(x, "core", [(0, 1), (1, 0)])


def exchange(x, axis):
    return lax.all_to_all(x, axis, 0, 0, tiled=False)


def total_of(x):
    parts = [x[i].astype(f32) for i in range(x.shape[0])]
    while len(parts) > 1:
        parts = [a + b for a, b in zip(parts[::2], parts[1::2])]
    return parts[0]


def gather(x, axis):
    n = lax.axis_size(axis)
    got = exchange(jnp.broadcast_to(x[None], (n,) + x.shape), axis)
    return got.reshape((n * x.shape[0],) + x.shape[1:])


def pair(own, other, place, axis):
    return jnp.where(
        place == 0,
        jnp.concatenate([own, other], axis),
        jnp.concatenate([other, own], axis),
    )


def per_device(tokens, up_weight, down_weight, out_grads):
    core, zl, rep = (lax.axis_index(a) for a in ("core", "zl", "rep"))
    rows, width = tokens.shape
    half = up_weight.shape[1] // 2
    n_row, n_zh, n_rep = (lax.axis_size(a) for a in ("row", "zh", "rep"))
    n_z = 2 * n_zh
    mine, theirs = core * half, (1 - core) * half

    even = [(p, p ^ 1) for p in range(n_z)]
    odd = [(p, (p + 1 if p % 2 else p - 1) % n_z) for p in range(n_z)]
    near = [(r, r ^ 1) for r in range(n_rep)]
    far = [(r, n_rep - 1 - r) for r in range(n_rep)]

    def z_swap(x, pairs):
        return lax.ppermute(x, ("zh", "zl"), pairs)

    def pick(x, index):
        return lax.dynamic_index_in_dim(x, index, 0, False)

    def plus(a, b):
        return (a.astype(f32) + b.astype(f32)).astype(bf16)

    up_keep = lax.dynamic_slice_in_dim(up_weight, mine, half, 1)
    up_other = swap(lax.dynamic_slice_in_dim(up_weight, theirs, half, 1))
    down_keep = lax.dynamic_slice_in_dim(down_weight, mine, half, 0)
    down_other = swap(lax.dynamic_slice_in_dim(down_weight, theirs, half, 0))
    up = jnp.concatenate([up_keep, up_other], 0)
    down = jnp.concatenate([down_keep, down_other], 1)

    own = gather(jnp.concatenate([tokens, out_grads], 1), "row")
    own, up, down = barrier((own, up, down))
    other = swap(own)
    total = own.shape[0]
    same, share = total // 2, total // n_z

    def columns_of(x, place):
        x = pick(x.reshape(2, same, 2 * width), place)
        return x[:, :width], x[:, width:]

    def rows_of(place):
        (t0, g0), (t1, g1) = columns_of(own, place), columns_of(other, place)
        return jnp.concatenate([t0, t1], 1), jnp.concatenate([g0, g1], 1)

    tok_send, og_send = rows_of(1 - zl)
    tok_keep, og_keep = rows_of(zl)

    hid_send = dot(tok_send, up, (1, 0))
    ag_send = dot(og_send, down, (1, 1))
    hid_send, ag_send, tok_keep, og_keep = barrier(
        (hid_send, ag_send, tok_keep, og_keep)
    )
    tok = jnp.concatenate([tok_keep, tok_send], 0)
    og = jnp.concatenate([og_keep, og_send], 0)
    hid_half = plus(dot(tok_keep, up, (1, 0)), z_swap(hid_send, even))
    ag_half = plus(dot(og_keep, down, (1, 1)), z_swap(ag_send, odd))
    halves = jnp.concatenate([hid_half, ag_half], 1).reshape(n_zh, share, 2 * half)
    sums = total_of(exchange(halves, "zh"))
    hidden, act_grads = sums[:, :half], sums[:, half:]
    act = jax.nn.gelu(hidden).astype(bf16)
    hid_grads = gelu_pullback(hidden, act_grads).astype(bf16)

    both = lax.all_gather(
        jnp.concatenate([act, hid_grads], 1), "zh", axis=0, tiled=True
    )

    act_half, hg_half = both[:, :half], both[:, half:]
    act_got, hg_got = z_swap(act_half, even), z_swap(hg_half, odd)
    act = jnp.concatenate([act_half, act_got], 0)
    hg = jnp.concatenate([hg_half, hg_got], 0)

    def scatter(x, axis, bit, pairs):
        def at(place):
            return lax.dynamic_index_in_dim(x, place, axis, False)

        return plus(at(bit), lax.ppermute(at(1 - bit), "rep", pairs))

    turn, high = (rep + 1) // 2 % 2, rep // 2
    down_part = dot(act, og, (0, 0)).reshape(2, half // 2, 2 * width)
    cut = width // 2
    order = [tok[:, i * cut : (i + 1) * cut] for i in (0, 2, 1, 3)]
    up_part = dot(jnp.concatenate(order, 1), hg, (0, 0)).reshape(2, width, half)
    down_part = scatter(down_part, 0, turn, near)
    down_part, act_half, act_got, hg_half, hg_got = barrier(
        (down_part, act_half, act_got, hg_half, hg_got)
    )
    act, hg = pair(act_half, act_got, zl, 0), pair(hg_half, hg_got, zl, 0)

    def output(columns):
        block = dot(act, down[:, columns], (1, 0))
        token = dot(hg, up[columns], (1, 1))
        return jnp.concatenate([block, token], 1)

    send = output(slice(width, None))
    up_keep, up_got = pick(up_part, high), lax.ppermute(
        pick(up_part, 1 - high), "rep", far
    )
    up_got, send, keep = barrier((up_got, send, output(slice(width))))
    up_part = plus(up_keep, up_got)
    down_part = plus(down_part, lax.ppermute(down_part, "rep", far))
    up_part = plus(up_part, lax.ppermute(up_part, "rep", near))
    down_own, down_got = down_part[:, :width], swap(down_part[:, width:])
    down_part = pair(down_own[None], down_got[None], core, 0)
    down_part = pair(down_part, lax.ppermute(down_part, "rep", near), turn, 1)
    down_grads = down_part.reshape(2 * half, width)
    up_part = pair(up_part[:cut], swap(up_part[cut:]), core, 1)
    up_grads = pair(up_part, lax.ppermute(up_part, "rep", far), high, 0)

    out = plus(keep, swap(send))
    out = total_of(exchange(out.reshape(n_row, rows, 2 * width), "row")).astype(bf16)
    return (out[:, :width], out[:, width:], up_grads, down_grads)


def solution(mesh):
    n_row, n_col, n_rep = mesh.devices.shape
    split = Mesh(
        mesh.devices.reshape(n_row, n_col // 4, 2, 2, n_rep),
        ("row", "zh", "zl", "core", "rep"),
    )
    col = ("zh", "zl", "core")
    acts = P(("rep", "row"), col)
    up = P(col, "row")
    down = P("row", col)
    return jax.shard_map(
        per_device,
        mesh=split,
        in_specs=(acts, up, down, acts),
        out_specs=(acts, acts, up, down),
        check_vma=False,
    )
```

```python
import jax
import jax.numpy as jnp
from jax import lax
from jax.sharding import Mesh, PartitionSpec as P

bf16 = jnp.bfloat16
f32 = jnp.float32
barrier = lax.optimization_barrier


def gelu_pullback(hidden, upstream):
    _, pullback = jax.vjp(jax.nn.gelu, hidden)
    return pullback(upstream)[0]


def dot(left, right, dims):
    return lax.dot_general(
        left, right, ((dims[:1], dims[1:]), ((), ())), preferred_element_type=f32
    ).astype(bf16)


def swap(x):
    return lax.ppermute(x, "core", [(0, 1), (1, 0)])


def exchange(x, axis):
    return lax.all_to_all(x, axis, 0, 0, tiled=False)


def total_of(x):
    parts = [x[i].astype(f32) for i in range(x.shape[0])]
    while len(parts) > 1:
        parts = [a + b for a, b in zip(parts[::2], parts[1::2])]
    return parts[0]


def gather(x, axis):
    n = lax.axis_size(axis)
    got = exchange(jnp.broadcast_to(x[None], (n,) + x.shape), axis)
    return got.reshape((n * x.shape[0],) + x.shape[1:])


def pair(own, other, place, axis):
    return jnp.where(
        place == 0,
        jnp.concatenate([own, other], axis),
        jnp.concatenate([other, own], axis),
    )


def per_device(tokens, up_weight, down_weight, out_grads):
    core, zl, rep = (lax.axis_index(a) for a in ("core", "zl", "rep"))
    rows, width = tokens.shape
    half = up_weight.shape[1] // 2
    n_row, n_zh, n_rep = (lax.axis_size(a) for a in ("row", "zh", "rep"))
    n_z = 2 * n_zh
    mine, theirs = core * half, (1 - core) * half

    even = [(p, p ^ 1) for p in range(n_z)]
    odd = [(p, (p + 1 if p % 2 else p - 1) % n_z) for p in range(n_z)]
    near = [(r, r ^ 1) for r in range(n_rep)]
    far = [(r, n_rep - 1 - r) for r in range(n_rep)]

    def z_swap(x, pairs):
        return lax.ppermute(x, ("zh", "zl"), pairs)

    def pick(x, index):
        return lax.dynamic_index_in_dim(x, index, 0, False)

    def plus(a, b):
        return (a.astype(f32) + b.astype(f32)).astype(bf16)

    up_keep = lax.dynamic_slice_in_dim(up_weight, mine, half, 1)
    up_other = swap(lax.dynamic_slice_in_dim(up_weight, theirs, half, 1))
    down_keep = lax.dynamic_slice_in_dim(down_weight, mine, half, 0)
    down_other = swap(lax.dynamic_slice_in_dim(down_weight, theirs, half, 0))
    up = jnp.concatenate([up_keep, up_other], 0)
    down = jnp.concatenate([down_keep, down_other], 1)

    own = gather(jnp.concatenate([tokens, out_grads], 1), "row")
    own, up, down = barrier((own, up, down))
    other = swap(own)
    total = own.shape[0]
    same, share = total // 2, total // n_z

    def columns_of(x, place):
        x = pick(x.reshape(2, same, 2 * width), place)
        return x[:, :width], x[:, width:]

    def rows_of(place):
        (t0, g0), (t1, g1) = columns_of(own, place), columns_of(other, place)
        return jnp.concatenate([t0, t1], 1), jnp.concatenate([g0, g1], 1)

    tok_send, og_send = rows_of(1 - zl)
    tok_keep, og_keep = rows_of(zl)

    hid_send = dot(tok_send, up, (1, 0))
    ag_send = dot(og_send, down, (1, 1))
    hid_send, ag_send, tok_keep, og_keep = barrier(
        (hid_send, ag_send, tok_keep, og_keep)
    )
    tok = jnp.concatenate([tok_keep, tok_send], 0)
    og = jnp.concatenate([og_keep, og_send], 0)
    hid_half = plus(dot(tok_keep, up, (1, 0)), z_swap(hid_send, even))
    ag_half = plus(dot(og_keep, down, (1, 1)), z_swap(ag_send, odd))
    halves = jnp.concatenate([hid_half, ag_half], 1).reshape(n_zh, share, 2 * half)
    sums = total_of(exchange(halves, "zh"))
    hidden, act_grads = sums[:, :half], sums[:, half:]
    act = jax.nn.gelu(hidden).astype(bf16)
    hid_grads = gelu_pullback(hidden, act_grads).astype(bf16)

    both = lax.all_gather(
        jnp.concatenate([act, hid_grads], 1), "zh", axis=0, tiled=True
    )

    act_half, hg_half = both[:, :half], both[:, half:]
    act_got, hg_got = z_swap(act_half, even), z_swap(hg_half, odd)
    act = jnp.concatenate([act_half, act_got], 0)
    hg = jnp.concatenate([hg_half, hg_got], 0)

    def scatter(x, axis, bit, pairs):
        def at(place):
            return lax.dynamic_index_in_dim(x, place, axis, False)

        return plus(at(bit), lax.ppermute(at(1 - bit), "rep", pairs))

    turn, high = (rep + 1) // 2 % 2, rep // 2
    down_part = dot(act, og, (0, 0)).reshape(2, half // 2, 2 * width)
    down_part = scatter(down_part, 0, turn, near)
    down_part, act_half, act_got, hg_half, hg_got = barrier(
        (down_part, act_half, act_got, hg_half, hg_got)
    )
    cut = width // 2
    order = [tok[:, i * cut : (i + 1) * cut] for i in (0, 2, 1, 3)]
    up_part = dot(jnp.concatenate(order, 1), hg, (0, 0)).reshape(2, width, half)
    up_got = lax.ppermute(pick(up_part, 1 - high), "rep", far)
    down_own, down_got = down_part[:, :width], swap(down_part[:, width:])
    down_got, up_got = barrier((down_got, up_got))
    up_part = plus(pick(up_part, high), up_got)
    down_part = pair(down_own[None], down_got[None], core, 0)
    down_part = plus(down_part, lax.ppermute(down_part, "rep", far))
    up_part = plus(up_part, lax.ppermute(up_part, "rep", near))
    down_part = pair(down_part, lax.ppermute(down_part, "rep", near), turn, 1)
    down_grads = down_part.reshape(2 * half, width)
    up_part = pair(up_part[:cut], swap(up_part[cut:]), core, 1)
    up_grads = pair(up_part, lax.ppermute(up_part, "rep", far), high, 0)

    act, hg = pair(act_half, act_got, zl, 0), pair(hg_half, hg_got, zl, 0)

    def output(columns):
        block = dot(act, down[:, columns], (1, 0))
        token = dot(hg, up[columns], (1, 1))
        return jnp.concatenate([block, token], 1)

    send = output(slice(width, None))
    out = plus(output(slice(width)), swap(send))
    out = total_of(exchange(out.reshape(n_row, rows, 2 * width), "row")).astype(bf16)
    return (out[:, :width], out[:, width:], up_grads, down_grads)


def solution(mesh):
    n_row, n_col, n_rep = mesh.devices.shape
    split = Mesh(
        mesh.devices.reshape(n_row, n_col // 4, 2, 2, n_rep),
        ("row", "zh", "zl", "core", "rep"),
    )
    col = ("zh", "zl", "core")
    acts = P(("rep", "row"), col)
    up = P(col, "row")
    down = P("row", col)
    return jax.shard_map(
        per_device,
        mesh=split,
        in_specs=(acts, up, down, acts),
        out_specs=(acts, acts, up, down),
        check_vma=False,
    )
```

```python
import jax
import jax.numpy as jnp
from jax import lax
from jax.sharding import Mesh, PartitionSpec as P

bf16 = jnp.bfloat16
f32 = jnp.float32
barrier = lax.optimization_barrier


def gelu_pullback(hidden, upstream):
    _, pullback = jax.vjp(jax.nn.gelu, hidden)
    return pullback(upstream)[0]


def dot(left, right, dims):
    return lax.dot_general(
        left, right, ((dims[:1], dims[1:]), ((), ())), preferred_element_type=f32
    ).astype(bf16)


def swap(x):
    return lax.ppermute(x, "core", [(0, 1), (1, 0)])


def exchange(x, axis):
    return lax.all_to_all(x, axis, 0, 0, tiled=False)


def total_of(x):
    parts = [x[i].astype(f32) for i in range(x.shape[0])]
    while len(parts) > 1:
        parts = [a + b for a, b in zip(parts[::2], parts[1::2])]
    return parts[0]


def gather(x, axis):
    n = lax.axis_size(axis)
    got = exchange(jnp.broadcast_to(x[None], (n,) + x.shape), axis)
    return got.reshape((n * x.shape[0],) + x.shape[1:])


def pair(own, other, place, axis):
    return jnp.where(
        place == 0,
        jnp.concatenate([own, other], axis),
        jnp.concatenate([other, own], axis),
    )


def per_device(tokens, up_weight, down_weight, out_grads):
    core, zl, rep = (lax.axis_index(a) for a in ("core", "zl", "rep"))
    rows, width = tokens.shape
    half = up_weight.shape[1] // 2
    n_row, n_zh, n_rep = (lax.axis_size(a) for a in ("row", "zh", "rep"))
    n_z = 2 * n_zh
    mine, theirs = core * half, (1 - core) * half

    even = [(p, p ^ 1) for p in range(n_z)]
    odd = [(p, (p + 1 if p % 2 else p - 1) % n_z) for p in range(n_z)]
    near = [(r, r ^ 1) for r in range(n_rep)]
    far = [(r, n_rep - 1 - r) for r in range(n_rep)]

    def z_swap(x, pairs):
        return lax.ppermute(x, ("zh", "zl"), pairs)

    def pick(x, index):
        return lax.dynamic_index_in_dim(x, index, 0, False)

    def plus(a, b):
        return (a.astype(f32) + b.astype(f32)).astype(bf16)

    up_keep = lax.dynamic_slice_in_dim(up_weight, mine, half, 1)
    up_other = swap(lax.dynamic_slice_in_dim(up_weight, theirs, half, 1))
    down_keep = lax.dynamic_slice_in_dim(down_weight, mine, half, 0)
    down_other = swap(lax.dynamic_slice_in_dim(down_weight, theirs, half, 0))
    up = jnp.concatenate([up_keep, up_other], 0)
    down = jnp.concatenate([down_keep, down_other], 1)

    own = gather(jnp.concatenate([tokens, out_grads], 1), "row")
    own, up, down = barrier((own, up, down))
    other = swap(own)
    total = own.shape[0]
    same, share = total // 2, total // n_z

    def columns_of(x, place):
        x = pick(x.reshape(2, same, 2 * width), place)
        return x[:, :width], x[:, width:]

    def rows_of(place):
        (t0, g0), (t1, g1) = columns_of(own, place), columns_of(other, place)
        return jnp.concatenate([t0, t1], 1), jnp.concatenate([g0, g1], 1)

    tok_send, og_send = rows_of(1 - zl)
    tok_keep, og_keep = rows_of(zl)

    hid_send = dot(tok_send, up, (1, 0))
    ag_send = dot(og_send, down, (1, 1))
    hid_send, ag_send, tok_keep, og_keep = barrier(
        (hid_send, ag_send, tok_keep, og_keep)
    )
    tok = jnp.concatenate([tok_keep, tok_send], 0)
    og = jnp.concatenate([og_keep, og_send], 0)
    hid_half = plus(dot(tok_keep, up, (1, 0)), z_swap(hid_send, even))
    ag_half = plus(dot(og_keep, down, (1, 1)), z_swap(ag_send, odd))
    halves = jnp.concatenate([hid_half, ag_half], 1).reshape(n_zh, share, 2 * half)
    sums = total_of(exchange(halves, "zh"))
    hidden, act_grads = sums[:, :half], sums[:, half:]
    act = jax.nn.gelu(hidden).astype(bf16)
    hid_grads = gelu_pullback(hidden, act_grads).astype(bf16)

    both = lax.all_gather(
        jnp.concatenate([act, hid_grads], 1), "zh", axis=0, tiled=True
    )

    act_half, hg_half = both[:, :half], both[:, half:]
    act_got, hg_got = z_swap(act_half, even), z_swap(hg_half, odd)
    act = jnp.concatenate([act_half, act_got], 0)
    hg = jnp.concatenate([hg_half, hg_got], 0)

    def scatter(x, axis, bit, pairs):
        def at(place):
            return lax.dynamic_index_in_dim(x, place, axis, False)

        return plus(at(bit), lax.ppermute(at(1 - bit), "rep", pairs))

    turn, high = (rep + 1) // 2 % 2, rep // 2
    down_part = dot(act, og, (0, 0)).reshape(2, half // 2, 2 * width)
    down_part = scatter(down_part, 0, turn, near)
    down_part, act_half, act_got, hg_half, hg_got = barrier(
        (down_part, act_half, act_got, hg_half, hg_got)
    )
    cut = width // 2
    order = [tok[:, i * cut : (i + 1) * cut] for i in (0, 2, 1, 3)]
    up_part = dot(jnp.concatenate(order, 1), hg, (0, 0)).reshape(2, width, half)
    up_got = lax.ppermute(pick(up_part, 1 - high), "rep", far)

    act, hg = pair(act_half, act_got, zl, 0), pair(hg_half, hg_got, zl, 0)

    def output(columns):
        block = dot(act, down[:, columns], (1, 0))
        token = dot(hg, up[columns], (1, 1))
        return jnp.concatenate([block, token], 1)

    send = output(slice(width, None))
    up_got, send = barrier((up_got, send))
    up_part = plus(pick(up_part, high), up_got)
    down_part = plus(down_part, lax.ppermute(down_part, "rep", far))
    up_part = plus(up_part, lax.ppermute(up_part, "rep", near))
    down_own, down_got = down_part[:, :width], swap(down_part[:, width:])
    down_part = pair(down_own[None], down_got[None], core, 0)
    down_part = pair(down_part, lax.ppermute(down_part, "rep", near), turn, 1)
    down_grads = down_part.reshape(2 * half, width)
    up_part = pair(up_part[:cut], swap(up_part[cut:]), core, 1)
    up_grads = pair(up_part, lax.ppermute(up_part, "rep", far), high, 0)

    out = plus(output(slice(width)), swap(send))
    out = total_of(exchange(out.reshape(n_row, rows, 2 * width), "row")).astype(bf16)
    return (out[:, :width], out[:, width:], up_grads, down_grads)


def solution(mesh):
    n_row, n_col, n_rep = mesh.devices.shape
    split = Mesh(
        mesh.devices.reshape(n_row, n_col // 4, 2, 2, n_rep),
        ("row", "zh", "zl", "core", "rep"),
    )
    col = ("zh", "zl", "core")
    acts = P(("rep", "row"), col)
    up = P(col, "row")
    down = P("row", col)
    return jax.shard_map(
        per_device,
        mesh=split,
        in_specs=(acts, up, down, acts),
        out_specs=(acts, acts, up, down),
        check_vma=False,
    )
```

```python
import jax
import jax.numpy as jnp
from jax import lax
from jax.sharding import Mesh, PartitionSpec as P

bf16 = jnp.bfloat16
f32 = jnp.float32
barrier = lax.optimization_barrier


def gelu_pullback(hidden, upstream):
    _, pullback = jax.vjp(jax.nn.gelu, hidden)
    return pullback(upstream)[0]


def dot(left, right, dims):
    return lax.dot_general(
        left, right, ((dims[:1], dims[1:]), ((), ())), preferred_element_type=f32
    ).astype(bf16)


def swap(x):
    return lax.ppermute(x, "core", [(0, 1), (1, 0)])


def exchange(x, axis):
    return lax.all_to_all(x, axis, 0, 0, tiled=False)


def total_of(x):
    parts = [x[i].astype(f32) for i in range(x.shape[0])]
    while len(parts) > 1:
        parts = [a + b for a, b in zip(parts[::2], parts[1::2])]
    return parts[0]


def gather(x, axis):
    n = lax.axis_size(axis)
    got = exchange(jnp.broadcast_to(x[None], (n,) + x.shape), axis)
    return got.reshape((n * x.shape[0],) + x.shape[1:])


def pair(own, other, place, axis):
    return jnp.where(
        place == 0,
        jnp.concatenate([own, other], axis),
        jnp.concatenate([other, own], axis),
    )


def per_device(tokens, up_weight, down_weight, out_grads):
    core, zl, rep = (lax.axis_index(a) for a in ("core", "zl", "rep"))
    rows, width = tokens.shape
    half = up_weight.shape[1] // 2
    n_row, n_zh, n_rep = (lax.axis_size(a) for a in ("row", "zh", "rep"))
    n_z = 2 * n_zh
    mine, theirs = core * half, (1 - core) * half

    even = [(p, p ^ 1) for p in range(n_z)]
    odd = [(p, (p + 1 if p % 2 else p - 1) % n_z) for p in range(n_z)]
    near = [(r, r ^ 1) for r in range(n_rep)]
    far = [(r, n_rep - 1 - r) for r in range(n_rep)]

    def z_swap(x, pairs):
        return lax.ppermute(x, ("zh", "zl"), pairs)

    def pick(x, index):
        return lax.dynamic_index_in_dim(x, index, 0, False)

    def plus(a, b):
        return (a.astype(f32) + b.astype(f32)).astype(bf16)

    up_keep = lax.dynamic_slice_in_dim(up_weight, mine, half, 1)
    up_other = swap(lax.dynamic_slice_in_dim(up_weight, theirs, half, 1))
    down_keep = lax.dynamic_slice_in_dim(down_weight, mine, half, 0)
    down_other = swap(lax.dynamic_slice_in_dim(down_weight, theirs, half, 0))
    up = jnp.concatenate([up_keep, up_other], 0)
    down = jnp.concatenate([down_keep, down_other], 1)

    own = lax.all_gather(
        jnp.concatenate([tokens, out_grads], 1), "row", axis=0, tiled=True
    )
    own, up, down = barrier((own, up, down))
    other = swap(own)
    total = own.shape[0]
    same, share = total // 2, total // n_z

    def columns_of(x, place):
        x = pick(x.reshape(2, same, 2 * width), place)
        return x[:, :width], x[:, width:]

    def rows_of(place):
        (t0, g0), (t1, g1) = columns_of(own, place), columns_of(other, place)
        return jnp.concatenate([t0, t1], 1), jnp.concatenate([g0, g1], 1)

    tok_send, og_send = rows_of(1 - zl)
    tok_keep, og_keep = rows_of(zl)

    hid_send = dot(tok_send, up, (1, 0))
    ag_send = dot(og_send, down, (1, 1))
    hid_send, ag_send, tok_keep, og_keep = barrier(
        (hid_send, ag_send, tok_keep, og_keep)
    )
    tok = jnp.concatenate([tok_keep, tok_send], 0)
    og = jnp.concatenate([og_keep, og_send], 0)
    hid_half = plus(dot(tok_keep, up, (1, 0)), z_swap(hid_send, even))
    ag_half = plus(dot(og_keep, down, (1, 1)), z_swap(ag_send, odd))
    halves = jnp.concatenate([hid_half, ag_half], 1).reshape(n_zh, share, 2 * half)
    sums = total_of(exchange(halves, "zh"))
    hidden, act_grads = sums[:, :half], sums[:, half:]
    act = jax.nn.gelu(hidden).astype(bf16)
    hid_grads = gelu_pullback(hidden, act_grads).astype(bf16)

    both = lax.all_gather(
        jnp.concatenate([act, hid_grads], 1), "zh", axis=0, tiled=True
    )

    act_half, hg_half = both[:, :half], both[:, half:]
    act_got, hg_got = z_swap(act_half, even), z_swap(hg_half, odd)
    act = jnp.concatenate([act_half, act_got], 0)
    hg = jnp.concatenate([hg_half, hg_got], 0)

    def scatter(x, axis, bit, pairs):
        def at(place):
            return lax.dynamic_index_in_dim(x, place, axis, False)

        return plus(at(bit), lax.ppermute(at(1 - bit), "rep", pairs))

    turn, high = (rep + 1) // 2 % 2, rep // 2
    down_part = dot(act, og, (0, 0)).reshape(2, half // 2, 2 * width)
    down_part = scatter(down_part, 0, turn, near)
    down_part, act_half, act_got, hg_half, hg_got = barrier(
        (down_part, act_half, act_got, hg_half, hg_got)
    )
    cut = width // 2
    order = [tok[:, i * cut : (i + 1) * cut] for i in (0, 2, 1, 3)]
    up_part = dot(jnp.concatenate(order, 1), hg, (0, 0)).reshape(2, width, half)
    up_got = lax.ppermute(pick(up_part, 1 - high), "rep", far)

    act, hg = pair(act_half, act_got, zl, 0), pair(hg_half, hg_got, zl, 0)

    def output(columns):
        block = dot(act, down[:, columns], (1, 0))
        token = dot(hg, up[columns], (1, 1))
        return jnp.concatenate([block, token], 1)

    send = output(slice(width, None))
    up_got, send = barrier((up_got, send))
    up_part = plus(pick(up_part, high), up_got)
    down_part = plus(down_part, lax.ppermute(down_part, "rep", far))
    up_part = plus(up_part, lax.ppermute(up_part, "rep", near))
    down_own, down_got = down_part[:, :width], swap(down_part[:, width:])
    down_part = pair(down_own[None], down_got[None], core, 0)
    down_part = pair(down_part, lax.ppermute(down_part, "rep", near), turn, 1)
    down_grads = down_part.reshape(2 * half, width)
    up_part = pair(up_part[:cut], swap(up_part[cut:]), core, 1)
    up_grads = pair(up_part, lax.ppermute(up_part, "rep", far), high, 0)

    out = plus(output(slice(width)), swap(send))
    out = total_of(exchange(out.reshape(n_row, rows, 2 * width), "row")).astype(bf16)
    return (out[:, :width], out[:, width:], up_grads, down_grads)


def solution(mesh):
    n_row, n_col, n_rep = mesh.devices.shape
    split = Mesh(
        mesh.devices.reshape(n_row, n_col // 4, 2, 2, n_rep),
        ("row", "zh", "zl", "core", "rep"),
    )
    col = ("zh", "zl", "core")
    acts = P(("rep", "row"), col)
    up = P(col, "row")
    down = P("row", col)
    return jax.shard_map(
        per_device,
        mesh=split,
        in_specs=(acts, up, down, acts),
        out_specs=(acts, acts, up, down),
        check_vma=False,
    )
```
